256 devices in a mesh: ens: 8 (over y, z_lo), node: 32 (over z_hi, x, core).
Axes of the slice: x: 4, y: 4, z: 8 (z_hi: 4, z_lo: 2; z = z_hi * 2 + z_lo), core: 2. Of those that a mesh axis runs over, the one named last changes fastest.
Arguments:
- hidden_embedding: bfloat16 [8, 32768, 1024], P('ens', 'node'), may hold values from -6 to 6
- random_perturbation: bfloat16 [8, 1024], P('ens'), may hold values from -3 to 3
- norm_gain: float32 [1024], replicated, may hold values from 0.5 to 1.5
- w_qkv: bfloat16 [1024, 3072], replicated, may hold values from -40 to 40
- w_proj: bfloat16 [1024, 1024], replicated, may hold values from -0.1875 to 0.1875
- w_fields: bfloat16 [1024, 100], replicated, may hold values from -0.1875 to 0.1875
- observed_reality: float32 [100, 32768], P(None, 'node'), may hold values from -6 to 6
- counts: int32 [32], replicated, may hold values from 512 to 1024, as said below
Outputs:
- predicted_outputs: bfloat16 [8, 100, 32768], P('ens', None, 'node')
- probabilistic_score: float32 [100, 32768], P(None, 'node')
- scaled_derivative: float32 [8, 100, 32768], P('ens', None, 'node')
The draws below stay inside these ranges and needn't reach their ends.
Inputs may be any that keep to these rules, and one draw needn't show every extreme that they name: `counts`: each shard has at least half of its 1024 slots live, its live nodes come first, one shard is full and one is exactly half full.
All inputs are finite; a program needn't handle non-finite values.
Results may differ from the reference program's by a relative error of at most 0.013.
The reference program's roundings to bfloat16 on the way count: a program that leaves them out, or rounds other values in their place, can miss the bound.
Values may be sent and summed in bfloat16 or wider, within the bound.
A program may use at most 128 MiB of HBM per device.

```python
import jax
import jax.numpy as jnp
from jax import lax

C = 1024
HEADS = 16
HEAD_GROUP = 4
VARS = 100
NODE_SLOTS = 1024
HALF_WINDOW = 256
MEMBERS = 8
NODES = 32768
N_NODE = 32


def draw_counts(key, part):
    first, second, third = jax.random.split(jax.random.fold_in(key, 17), 3)
    values = jax.random.randint(first, (N_NODE,), NODE_SLOTS // 2, NODE_SLOTS + 1)
    full_at = jax.random.randint(second, (), 0, N_NODE)
    half_at = (full_at + 1 + jax.random.randint(third, (), 0, N_NODE - 1)) % N_NODE
    places = jnp.arange(N_NODE, dtype=jnp.int32)
    values = jnp.where(places == full_at, NODE_SLOTS, values)
    values = jnp.where(places == half_at, NODE_SLOTS // 2, values)
    return values.astype(jnp.int32)


def draw_hidden_embedding(key, part):
    first = jax.random.fold_in(jax.random.fold_in(key, 29), 0)
    base = jax.random.truncated_normal(first, -6.0, 6.0, (MEMBERS, NODES, C), jnp.float32)
    return base.astype(jnp.bfloat16)


def draw_w_qkv(key, part):
    first = jax.random.fold_in(jax.random.fold_in(key, 41), 0)
    scale = jnp.float32(C) ** (-0.5)
    whole = jax.random.truncated_normal(first, -6.0, 6.0, (C, 3 * C), jnp.float32) * scale
    return whole.astype(jnp.bfloat16)


def block_levels(key, shape, shards, low, largest):
    gain, own = 1.0, jax.random.fold_in(key, 6)
    for position, parts in shards:
        steps = jnp.exp(jax.random.uniform(jax.random.fold_in(own, position), (parts,), jnp.float32, low / len(shards), largest / len(shards)))
        gain = gain * jnp.repeat(steps, shape[position] // parts).reshape([-1 if axis == position else 1 for axis in range(len(shape))])
    return gain


def centred(key, dims, deviation, reach, cuts=(), held_as=jnp.bfloat16):
    values = deviation * jax.random.normal(key, dims, jnp.float32)
    if cuts:
        values = values * block_levels(key, dims, cuts, -0.22, 0.18)
    return jnp.clip(values, -reach, reach).astype(held_as)


def setup_inputs(seed: int = 0) -> dict:
    seeds = jax.random.split(jax.random.key(seed), 9)
    return {
        "hidden_embedding": draw_hidden_embedding(jax.random.fold_in(seeds[8], 71), 0),
        "random_perturbation": centred(seeds[1], (MEMBERS, C), 0.5, 3.0, ((0, 8),)),
        "norm_gain": jnp.clip(1.0 + 0.1 * jax.random.normal(seeds[2], (C,), jnp.float32), 0.5, 1.5),
        "w_qkv": draw_w_qkv(jax.random.fold_in(seeds[8], 71), 0),
        "w_proj": centred(seeds[4], (C, C), C ** -0.5, 0.1875),
        "w_fields": centred(seeds[5], (C, VARS), C ** -0.5, 0.1875),
        "observed_reality": centred(seeds[6], (VARS, NODES), 1.0, 6.0, ((1, 32),), jnp.float32),
        "counts": draw_counts(jax.random.fold_in(seeds[8], 71), 0),
    }


smooth_sq = 0.01
alpha_fair = 0.95

def attend(query, keys, values, allowed, heads, group):
    mem, rows, window_width = query.shape
    keyn = keys.shape[1]
    head_dim = window_width // heads
    groups = heads // group

    def split(arr, count):
        return jnp.moveaxis(arr.reshape(mem, count, groups, group, head_dim), 2, 1).reshape(mem * groups, count, group, head_dim)

    def one_group(item):
        q_part, k_part, v_part = item
        scores = jnp.einsum('qhd,khd->hqk', q_part.astype(jnp.float32), k_part.astype(jnp.float32)) / jnp.sqrt(jnp.float32(head_dim))
        scores = jnp.where(allowed[None], scores, jnp.float32(-1e+30))
        top = lax.optimization_barrier(jnp.max(scores, axis=-1, keepdims=True))
        expd = jnp.exp(scores - top)
        probs = (expd / lax.optimization_barrier(jnp.sum(expd, axis=-1, keepdims=True))).astype(jnp.bfloat16)
        return jnp.einsum('hqk,khd->qhd', probs.astype(jnp.float32), v_part.astype(jnp.float32)).astype(jnp.bfloat16)
    out = lax.map(one_group, (split(query, rows), split(keys, keyn), split(values, keyn)))
    out = jnp.moveaxis(out.reshape(mem, groups, rows, group, head_dim), 1, 2)
    return out.reshape(mem, rows, window_width)

def score_fragments(gridded_quantities, observed_reality, valid_flags):
    total = gridded_quantities.shape[0]

    def pair(row):
        diff = row[None] - gridded_quantities
        absd = jnp.sqrt(diff * diff + smooth_sq)
        return (lax.optimization_barrier(jnp.sum(absd, axis=0)), lax.optimization_barrier(jnp.sum(diff / absd, axis=0)))
    pair_sum, pair_grad = lax.map(pair, gridded_quantities)
    dtruth = gridded_quantities - observed_reality[None]
    atruth = jnp.sqrt(dtruth * dtruth + smooth_sq)
    eps_fair = (1.0 - alpha_fair) / total
    probabilistic_score = valid_flags[None] * (lax.optimization_barrier(jnp.mean(atruth, axis=0)) - (1.0 - eps_fair) / (2.0 * total * (total - 1)) * (lax.optimization_barrier(jnp.sum(pair_sum, axis=0)) - total * jnp.sqrt(jnp.float32(smooth_sq))))
    scaled_derivative = valid_flags[None, None] * (dtruth / atruth - (1.0 - eps_fair) / (total - 1) * pair_grad)
    return (probabilistic_score, scaled_derivative)

def reference(hidden_embedding, random_perturbation, norm_gain, w_qkv, w_proj, w_fields, observed_reality, counts):
    window_width = hidden_embedding.shape[2]
    slots = jnp.arange(NODES, dtype=jnp.int32)
    valid_flags = (slots % NODE_SLOTS < counts[slots // NODE_SLOTS]).astype(jnp.float32)
    live_pad = jnp.pad(valid_flags, (HALF_WINDOW, HALF_WINDOW))

    def lone_realisation(item):
        xrow, nrow = item
        x32 = xrow.astype(jnp.float32)
        mean = lax.optimization_barrier(jnp.mean(x32, axis=-1, keepdims=True))
        var = lax.optimization_barrier(jnp.mean((x32 - mean) ** 2, axis=-1, keepdims=True))
        normed = ((x32 - mean) * lax.rsqrt(var + 1e-05) * norm_gain[None] * (1.0 + nrow.astype(jnp.float32))[None]).astype(jnp.bfloat16)
        query_key_value = jnp.dot(normed, w_qkv, preferred_element_type=jnp.float32).astype(jnp.bfloat16)
        query = query_key_value[:, :window_width]
        kpad = jnp.pad(query_key_value[:, window_width:2 * window_width], ((HALF_WINDOW, HALF_WINDOW), (0, 0)))
        value_padded = jnp.pad(query_key_value[:, 2 * window_width:], ((HALF_WINDOW, HALF_WINDOW), (0, 0)))
        rel = jnp.arange(NODE_SLOTS + 2 * HALF_WINDOW, dtype=jnp.int32)[None, :] - HALF_WINDOW - jnp.arange(NODE_SLOTS, dtype=jnp.int32)[:, None]

        def shard(index):
            start_index = (index * NODE_SLOTS).astype(jnp.int32)
            q_rows = lax.dynamic_slice_in_dim(query, start_index, NODE_SLOTS, 0)
            k_rows = lax.dynamic_slice_in_dim(kpad, start_index, NODE_SLOTS + 2 * HALF_WINDOW, 0)
            value_rows = lax.dynamic_slice_in_dim(value_padded, start_index, NODE_SLOTS + 2 * HALF_WINDOW, 0)
            key_live = lax.dynamic_slice_in_dim(live_pad, start_index, NODE_SLOTS + 2 * HALF_WINDOW, 0)
            allowed = (rel >= -HALF_WINDOW) & (rel < HALF_WINDOW) & ((key_live[None, :] > 0.5) | (rel == 0))
            return attend(q_rows[None], k_rows[None], value_rows[None], allowed, HEADS, HEAD_GROUP)[0]
        attended = lax.map(shard, jnp.arange(N_NODE, dtype=jnp.int32)).reshape(NODES, window_width)
        updated = (x32 + jnp.dot(attended, w_proj, preferred_element_type=jnp.float32)).astype(jnp.bfloat16)
        gridded_quantities = jnp.dot(updated, w_fields, preferred_element_type=jnp.float32)
        return (gridded_quantities * valid_flags[:, None]).astype(jnp.bfloat16).T
    predicted_outputs = lax.map(lone_realisation, (hidden_embedding, random_perturbation))
    probabilistic_score, scaled_derivative = score_fragments(predicted_outputs.astype(jnp.float32), observed_reality, valid_flags)
    return (predicted_outputs, probabilistic_score, scaled_derivative)
```

```python
import jax
import jax.numpy as jnp
from jax import lax
from jax.experimental import pallas as pl
from jax.experimental.pallas import tpu as pltpu
from jax.sharding import PartitionSpec as P

C = 1024
HEADS = 16
HEAD_DIM = 64
PAIRS = HEADS // 2
ROWS = 1024
BLOCK = 256
HALF = 128
EXT = ROWS + 2 * BLOCK
SPAN = 640
VARS = 100
VPAD = 112
MEMBERS = 8
V_ROWS = 80

SMOOTH_SQ = 0.01
ALPHA_FAIR = 0.95
EPS_FAIR = (1.0 - ALPHA_FAIR) / MEMBERS
LOG2E = 1.4426950408889634
MASKED = -1e30

F32 = jnp.float32
BF16 = jnp.bfloat16
NT = (((1,), (1,)), ((), ()))
MESH = pl.DeviceIdType.MESH


def aligned(index, width):
    return pl.ds(pl.multiple_of(index * width, width), width)


def normalise(x, scale_row):
    x32 = x.astype(F32)
    mean = jnp.mean(x32, axis=-1, keepdims=True)
    centred = x32 - mean
    var = jnp.mean(centred * centred, axis=-1, keepdims=True)
    return (centred * lax.rsqrt(var + 1e-5) * scale_row).astype(BF16)


def kernel(
    counts_ref,
    x_hbm,
    pert_ref,
    gain_ref,
    wqkv_hbm,
    wproj_hbm,
    wf_ref,
    obs_ref,
    pred_ref,
    score_ref,
    deriv_ref,
    x_ref,
    halo_ref,
    wqkv_ref,
    wproj_ref,
    wf_pad,
    normed_ref,
    q_ref,
    k_ref,
    vt_ref,
    bias_ref,
    s0,
    s1,
    p0,
    p1,
    m0,
    m1,
    att_ref,
    gat_ref,
    x_sem,
    w_sem,
    halo_send,
    halo_recv,
    out_send,
    out_recv,
):
    ens = lax.axis_index("ens")
    node = lax.axis_index("node")
    ens_size = MEMBERS
    nodes = lax.axis_size("node")
    left = (node + nodes - 1) % nodes
    right = (node + 1) % nodes

    barrier = pltpu.get_barrier_semaphore()
    for near in (left, right):
        pl.semaphore_signal(barrier, inc=1, device_id={"node": near}, device_id_type=MESH)
    for step in range(1, ens_size):
        pl.semaphore_signal(
            barrier, inc=1, device_id={"ens": (ens + step) % ens_size}, device_id_type=MESH
        )

    def x_copy(part):
        rows = pl.ds(part * BLOCK, BLOCK)
        return pltpu.make_async_copy(x_hbm.at[0, rows], x_ref.at[rows], x_sem.at[part])

    def w_copy(part):
        cols = pl.ds(part * C, C)
        return pltpu.make_async_copy(wqkv_hbm.at[:, cols], wqkv_ref.at[:, cols], w_sem.at[part])

    wproj_copy = pltpu.make_async_copy(wproj_hbm, wproj_ref, w_sem.at[3])
    for part in range(4):
        x_copy(part).start()
    for part in range(3):
        w_copy(part).start()
    wproj_copy.start()

    pl.semaphore_wait(barrier, ens_size + 1)

    to_left = pltpu.make_async_remote_copy(
        src_ref=x_hbm.at[0, pl.ds(0, BLOCK)],
        dst_ref=halo_ref.at[1],
        send_sem=halo_send.at[1],
        recv_sem=halo_recv.at[1],
        device_id={"node": left},
        device_id_type=MESH,
    )
    to_right = pltpu.make_async_remote_copy(
        src_ref=x_hbm.at[0, pl.ds(ROWS - BLOCK, BLOCK)],
        dst_ref=halo_ref.at[0],
        send_sem=halo_send.at[0],
        recv_sem=halo_recv.at[0],
        device_id={"node": right},
        device_id_type=MESH,
    )
    to_left.start()
    to_right.start()

    own_count = counts_ref[node]
    low_count = jnp.where(node > 0, counts_ref[(node + nodes - 1) % nodes], 0)
    high_count = jnp.where(node < nodes - 1, counts_ref[(node + 1) % nodes], 0)
    key = lax.broadcasted_iota(jnp.int32, (SPAN, HALF), 0)
    query = lax.broadcasted_iota(jnp.int32, (SPAN, HALF), 1)
    ahead = key - query
    in_window = (ahead >= 0) & (ahead < 2 * BLOCK)
    itself = ahead == BLOCK

    def make_bias(t, carry):
        place = key + t * HALF
        end = jnp.where(
            place < BLOCK,
            low_count - (ROWS - BLOCK),
            jnp.where(place < BLOCK + ROWS, own_count + BLOCK, high_count + (BLOCK + ROWS)),
        )
        allowed = in_window & ((place < end) | itself)
        bias_ref[t] = jnp.where(allowed, 0.0, MASKED)
        return carry

    lax.fori_loop(0, ROWS // HALF, make_bias, 0)
    p0[...] = jnp.zeros_like(p0)
    p1[...] = jnp.zeros_like(p1)
    row = lax.broadcasted_iota(jnp.int32, (V_ROWS - HEAD_DIM, EXT), 0)
    tail = jnp.where(row == 0, 1.0, 0.0).astype(BF16)
    for head in range(HEADS):
        vt_ref[head, HEAD_DIM:V_ROWS, :] = tail
    wf_pad[...] = jnp.zeros_like(wf_pad)
    wf_pad[:, :VARS] = wf_ref[...]

    scale_row = gain_ref[...] * (1.0 + pert_ref[...].astype(F32))

    for part in range(4):
        x_copy(part).wait()

    def norm_own(step, carry):
        rows = aligned(step, 64)
        normed_ref[rows] = normalise(x_ref[rows], scale_row)
        return carry

    lax.fori_loop(0, ROWS // 64, norm_own, 0)

    lane = lax.broadcasted_iota(jnp.int32, (HALF, HALF), 1)
    even_lane = lane < HEAD_DIM

    def put_q(q, pair):
        for b in range(ROWS // BLOCK):
            for g in range(2):
                part = q[b * BLOCK + g * HALF : b * BLOCK + (g + 1) * HALF]
                q_ref[b, pair, g, :HALF] = jnp.where(even_lane, part, 0.0).astype(BF16)
                q_ref[b, pair, g, HALF:] = jnp.where(even_lane, 0.0, part).astype(BF16)

    def put_v(v, pair, at):
        vt = jnp.transpose(v).astype(BF16)
        vt_ref[2 * pair, :HEAD_DIM, at] = vt[:HEAD_DIM]
        vt_ref[2 * pair + 1, :HEAD_DIM, at] = vt[HEAD_DIM:]

    w_copy(0).wait()

    def project_q(tile, carry):
        cols = aligned(tile, 256)
        acc = jnp.dot(normed_ref[...], wqkv_ref[:, cols], preferred_element_type=F32) * 0.125
        put_q(acc[:, :128], 2 * tile)
        put_q(acc[:, 128:], 2 * tile + 1)
        return carry

    lax.fori_loop(0, 4, project_q, 0)
    w_copy(1).wait()

    def project_k(tile, carry):
        cols = aligned(tile, 256)
        acc = jnp.dot(normed_ref[...], wqkv_ref[:, aligned(4 + tile, 256)], preferred_element_type=F32)
        k_ref[BLOCK : BLOCK + ROWS, cols] = acc.astype(BF16)
        return carry

    lax.fori_loop(0, 4, project_k, 0)
    w_copy(2).wait()

    def project_v(tile, carry):
        acc = jnp.dot(normed_ref[...], wqkv_ref[:, aligned(8 + tile, 256)], preferred_element_type=F32)
        at = pl.ds(BLOCK, ROWS)
        put_v(acc[:, :128], 2 * tile, at)
        put_v(acc[:, 128:], 2 * tile + 1, at)
        return carry

    lax.fori_loop(0, 4, project_v, 0)

    def halo_rows():
        to_left.wait_recv()
        to_right.wait_recv()

        def norm_halo(step, carry):
            rows = aligned(step, 64)
            normed_ref[rows] = normalise(halo_ref[step // 4, aligned(step % 4, 64)], scale_row)
            return carry

        lax.fori_loop(0, 8, norm_halo, 0)

        def project_halo(tile, carry):
            normed = normed_ref[: 2 * BLOCK]
            cols = aligned(tile, 256)
            acc = jnp.dot(normed, wqkv_ref[:, aligned(4 + tile, 256)], preferred_element_type=F32)
            k_ref[:BLOCK, cols] = acc[:BLOCK].astype(BF16)
            k_ref[BLOCK + ROWS :, cols] = acc[BLOCK:].astype(BF16)
            acc = jnp.dot(normed, wqkv_ref[:, aligned(8 + tile, 256)], preferred_element_type=F32)
            for half in range(2):
                part = acc[:, half * 128 : (half + 1) * 128]
                put_v(part[:BLOCK], 2 * tile + half, pl.ds(0, BLOCK))
                put_v(part[BLOCK:], 2 * tile + half, pl.ds(BLOCK + ROWS, BLOCK))
            return carry

        lax.fori_loop(0, 4, project_halo, 0)

    S = (s0, s1)
    PB = (p0, p1)
    M = (m0, m1)

    def scores(b, pair, slot, g):
        keys = k_ref[pl.ds(pl.multiple_of(b * BLOCK + g * HALF, HALF), SPAN), pair * 128 : (pair + 1) * 128]
        s = lax.dot_general(keys, q_ref[b, pair, g], NT, preferred_element_type=F32)
        bias = bias_ref[2 * b + g]
        s = s + jnp.concatenate([bias, bias], axis=1)
        S[slot][g] = s
        M[slot][g] = jnp.max(s.reshape(SPAN // 8, 8, 2 * HALF), axis=0)

    def weights(slot, g, h):
        lanes = slice(h * HALF, (h + 1) * HALF)
        top = jnp.max(M[slot][g, :, lanes], axis=0, keepdims=True)
        e = jnp.exp2((S[slot][g, :, lanes] - top) * LOG2E).astype(BF16)
        PB[slot][h, g * HALF : g * HALF + SPAN, g * HALF : (g + 1) * HALF] = e

    def mix(b, pair, slot):
        out = []
        for h in range(2):
            values = vt_ref[2 * pair + h, :, pl.ds(pl.multiple_of(b * BLOCK, BLOCK), 3 * BLOCK)]
            o = jnp.dot(values, PB[slot][h], preferred_element_type=F32)
            out.append(o[:HEAD_DIM] / o[HEAD_DIM : HEAD_DIM + 1])
        both = jnp.concatenate(out, axis=0)
        att_ref[:, pair * 128 : (pair + 1) * 128] = jnp.transpose(both).astype(BF16)

    def attend(b):
        for step in range(PAIRS + 2):
            if step >= 2:
                mix(b, step - 2, step % 2)
            if 1 <= step <= PAIRS:
                for g in range(2):
                    for h in range(2):
                        weights((step - 1) % 2, g, h)
            if step < PAIRS:
                for g in range(2):
                    scores(b, step, step % 2, g)

    def out_copy(order, b, step):
        return pltpu.make_async_remote_copy(
            src_ref=gat_ref.at[ens, b],
            dst_ref=gat_ref.at[ens, b],
            send_sem=out_send.at[order, step - 1],
            recv_sem=out_recv.at[order, step - 1],
            device_id={"ens": (ens + step) % ens_size},
            device_id_type=MESH,
        )

    def in_copy(order, b, step):
        source = (ens + ens_size - step) % ens_size
        return pltpu.make_async_remote_copy(
            src_ref=gat_ref.at[source, b],
            dst_ref=gat_ref.at[source, b],
            send_sem=out_send.at[order, step - 1],
            recv_sem=out_recv.at[order, step - 1],
            device_id={"ens": (ens + step) % ens_size},
            device_id_type=MESH,
        )

    def live_row(b):
        slot = lax.broadcasted_iota(jnp.int32, (1, BLOCK), 1) + b * BLOCK
        return jnp.where(slot < own_count, 1.0, 0.0)

    def decode(order, b):
        rows = aligned(b, BLOCK)
        mixed = jnp.dot(att_ref[...], wproj_ref[...], preferred_element_type=F32)
        updated = (x_ref[rows].astype(F32) + mixed).astype(BF16)
        fields = jnp.dot(updated, wf_pad[...], preferred_element_type=F32)
        fields = (jnp.transpose(fields) * live_row(b)).astype(BF16)
        gat_ref[ens, b] = fields[:VPAD]
        pred_ref[0, :, rows] = fields[:VARS]
        for step in range(1, ens_size):
            out_copy(order, b, step).start()

    def score_rows(b, start, count, live):
        cols = aligned(b, BLOCK)
        rows = pl.ds(start, count)
        tile = pl.ds(start, 16)
        f = [gat_ref[m, b, tile, :].astype(F32)[:count] for m in range(ens_size)]
        mine = gat_ref[ens, b, tile, :].astype(F32)[:count]
        truth = obs_ref[rows, cols]

        def size(d):
            square = d * d + SMOOTH_SQ
            inverse = lax.rsqrt(square)
            return square * inverse, inverse

        to_truth = size(f[0] - truth)[0]
        for m in range(1, ens_size):
            to_truth = to_truth + size(f[m] - truth)[0]
        spread = None
        for m in range(ens_size):
            for other in range(m):
                term = size(f[m] - f[other])[0]
                spread = term if spread is None else spread + term
        grad = None
        for other in range(ens_size):
            d = mine - f[other]
            term = d * size(d)[1]
            grad = term if grad is None else grad + term
        d = mine - truth
        pull = d * size(d)[1]
        score_ref[rows, cols] = live * (
            to_truth * (1.0 / ens_size)
            - ((1.0 - EPS_FAIR) / (ens_size * (ens_size - 1))) * spread
        )
        deriv_ref[0, rows, cols] = live * (pull - ((1.0 - EPS_FAIR) / (ens_size - 1)) * grad)

    def score(order, b):
        for step in range(1, ens_size):
            in_copy(order, b, step).wait_recv()
        live = live_row(b)

        def some(r, carry):
            score_rows(b, pl.multiple_of(r * 16, 16), 16, live)
            return carry

        lax.fori_loop(0, VARS // 16, some, 0)
        score_rows(b, (VARS // 16) * 16, VARS % 16, live)

    wproj_copy.wait()

    def block_at(order):
        return (order + 1) % 3 + 2 * (order // 3)

    def one_block(order, carry):
        b = block_at(order)

        @pl.when(order == 2)
        def _():
            halo_rows()

        attend(b)
        decode(order, b)

        @pl.when(order >= 2)
        def _():
            score(order - 2, block_at(order - 2))

        return carry

    lax.fori_loop(0, 4, one_block, 0)
    score(2, 0)
    score(3, 3)

    to_left.wait_send()
    to_right.wait_send()

    def sent(order, carry):
        for step in range(1, ens_size):
            out_copy(order, block_at(order), step).wait_send()
        return carry

    lax.fori_loop(0, 4, sent, 0)


def on_device(x, pert, gain, wqkv, wproj, wf, obs, counts):
    vmem = pl.BlockSpec(memory_space=pltpu.VMEM)
    smem = pl.BlockSpec(memory_space=pltpu.SMEM)
    hbm = pl.BlockSpec(memory_space=pl.ANY)
    dma = pltpu.SemaphoreType.DMA
    return pl.pallas_call(
        kernel,
        out_shape=(
            jax.ShapeDtypeStruct((1, VARS, ROWS), BF16),
            jax.ShapeDtypeStruct((VARS, ROWS), F32),
            jax.ShapeDtypeStruct((1, VARS, ROWS), F32),
        ),
        in_specs=[smem, hbm, vmem, vmem, hbm, hbm, vmem, vmem],
        out_specs=(vmem, vmem, vmem),
        scratch_shapes=[
            pltpu.VMEM((ROWS, C), BF16),
            pltpu.VMEM((2, BLOCK, C), BF16),
            pltpu.VMEM((C, 3 * C), BF16),
            pltpu.VMEM((C, C), BF16),
            pltpu.VMEM((C, 128), BF16),
            pltpu.VMEM((ROWS, C), BF16),
            pltpu.VMEM((4, PAIRS, 2, 2 * HALF, 128), BF16),
            pltpu.VMEM((EXT, C), BF16),
            pltpu.VMEM((HEADS, V_ROWS, EXT), BF16),
            pltpu.VMEM((ROWS // HALF, SPAN, HALF), F32),
            pltpu.VMEM((2, SPAN, 2 * HALF), F32),
            pltpu.VMEM((2, SPAN, 2 * HALF), F32),
            pltpu.VMEM((2, 3 * BLOCK, BLOCK), BF16),
            pltpu.VMEM((2, 3 * BLOCK, BLOCK), BF16),
            pltpu.VMEM((2, 8, 2 * HALF), F32),
            pltpu.VMEM((2, 8, 2 * HALF), F32),
            pltpu.VMEM((BLOCK, C), BF16),
            pltpu.VMEM((MEMBERS, 4, VPAD, BLOCK), BF16),
            dma((4,)),
            dma((4,)),
            dma((2,)),
            dma((2,)),
            dma((4, MEMBERS - 1)),
            dma((4, MEMBERS - 1)),
        ],
        compiler_params=pltpu.CompilerParams(
            collective_id=0, has_side_effects=True, vmem_limit_bytes=56 * 2**20
        ),
        cost_estimate=pl.CostEstimate(flops=20_000_000_000, bytes_accessed=14_000_000, transcendentals=13_000_000),
    )(counts, x, pert, gain.reshape(1, C), wqkv, wproj, wf, obs)


def solution(mesh):
    return jax.shard_map(
        on_device,
        mesh=mesh,
        in_specs=(P("ens", "node", None), P("ens", None), P(), P(), P(), P(), P(None, "node"), P()),
        out_specs=(P("ens", None, "node"), P(None, "node"), P("ens", None, "node")),
        check_vma=False,
    )
```

```python
import jax
import jax.numpy as jnp
from jax import lax
from jax.experimental import pallas as pl
from jax.experimental.pallas import tpu as pltpu
from jax.sharding import PartitionSpec as P

C = 1024
HEADS = 16
HEAD_DIM = 64
PAIRS = HEADS // 2
ROWS = 1024
BLOCK = 256
HALF = 128
EXT = ROWS + 2 * BLOCK
SPAN = 640
VARS = 100
VPAD = 112
MEMBERS = 8
V_ROWS = 80

SMOOTH_SQ = 0.01
ALPHA_FAIR = 0.95
EPS_FAIR = (1.0 - ALPHA_FAIR) / MEMBERS
LOG2E = 1.4426950408889634
MASKED = -1e30

F32 = jnp.float32
BF16 = jnp.bfloat16
NT = (((1,), (1,)), ((), ()))
MESH = pl.DeviceIdType.MESH


def aligned(index, width):
    return pl.ds(pl.multiple_of(index * width, width), width)


def normalise(x, scale_row):
    x32 = x.astype(F32)
    mean = jnp.mean(x32, axis=-1, keepdims=True)
    centred = x32 - mean
    var = jnp.mean(centred * centred, axis=-1, keepdims=True)
    return (centred * lax.rsqrt(var + 1e-5) * scale_row).astype(BF16)


def kernel(
    counts_ref,
    x_hbm,
    pert_ref,
    gain_ref,
    wqkv_hbm,
    wproj_hbm,
    wf_ref,
    obs_ref,
    pred_ref,
    score_ref,
    deriv_ref,
    x_ref,
    halo_ref,
    wqkv_ref,
    wproj_ref,
    wf_pad,
    normed_ref,
    q_ref,
    k_ref,
    vt_ref,
    bias_ref,
    s0,
    s1,
    p0,
    p1,
    m0,
    m1,
    att_ref,
    gat_ref,
    x_sem,
    w_sem,
    halo_send,
    halo_recv,
    out_send,
    out_recv,
):
    ens = lax.axis_index("ens")
    node = lax.axis_index("node")
    ens_size = MEMBERS
    nodes = lax.axis_size("node")
    left = (node + nodes - 1) % nodes
    right = (node + 1) % nodes

    barrier = pltpu.get_barrier_semaphore()
    for near in (left, right):
        pl.semaphore_signal(barrier, inc=1, device_id={"node": near}, device_id_type=MESH)
    for step in range(1, ens_size):
        pl.semaphore_signal(
            barrier, inc=1, device_id={"ens": (ens + step) % ens_size}, device_id_type=MESH
        )

    def x_copy(part):
        rows = pl.ds(part * BLOCK, BLOCK)
        return pltpu.make_async_copy(x_hbm.at[0, rows], x_ref.at[rows], x_sem.at[part])

    def w_copy(part):
        cols = pl.ds(part * C, C)
        return pltpu.make_async_copy(wqkv_hbm.at[:, cols], wqkv_ref.at[:, cols], w_sem.at[part])

    wproj_copy = pltpu.make_async_copy(wproj_hbm, wproj_ref, w_sem.at[3])
    for part in range(4):
        x_copy(part).start()

    pl.semaphore_wait(barrier, ens_size + 1)

    to_left = pltpu.make_async_remote_copy(
        src_ref=x_hbm.at[0, pl.ds(0, BLOCK)],
        dst_ref=halo_ref.at[1],
        send_sem=halo_send.at[1],
        recv_sem=halo_recv.at[1],
        device_id={"node": left},
        device_id_type=MESH,
    )
    to_right = pltpu.make_async_remote_copy(
        src_ref=x_hbm.at[0, pl.ds(ROWS - BLOCK, BLOCK)],
        dst_ref=halo_ref.at[0],
        send_sem=halo_send.at[0],
        recv_sem=halo_recv.at[0],
        device_id={"node": right},
        device_id_type=MESH,
    )
    to_left.start()
    to_right.start()

    own_count = counts_ref[node]
    low_count = jnp.where(node > 0, counts_ref[(node + nodes - 1) % nodes], 0)
    high_count = jnp.where(node < nodes - 1, counts_ref[(node + 1) % nodes], 0)
    key = lax.broadcasted_iota(jnp.int32, (SPAN, HALF), 0)
    query = lax.broadcasted_iota(jnp.int32, (SPAN, HALF), 1)
    ahead = key - query
    in_window = (ahead >= 0) & (ahead < 2 * BLOCK)
    itself = ahead == BLOCK

    def make_bias(t, carry):
        place = key + t * HALF
        end = jnp.where(
            place < BLOCK,
            low_count - (ROWS - BLOCK),
            jnp.where(place < BLOCK + ROWS, own_count + BLOCK, high_count + (BLOCK + ROWS)),
        )
        allowed = in_window & ((place < end) | itself)
        bias_ref[t] = jnp.where(allowed, 0.0, MASKED)
        return carry

    lax.fori_loop(0, ROWS // HALF, make_bias, 0)
    p0[...] = jnp.zeros_like(p0)
    p1[...] = jnp.zeros_like(p1)
    row = lax.broadcasted_iota(jnp.int32, (V_ROWS - HEAD_DIM, EXT), 0)
    tail = jnp.where(row == 0, 1.0, 0.0).astype(BF16)
    for head in range(HEADS):
        vt_ref[head, HEAD_DIM:V_ROWS, :] = tail
    wf_pad[...] = jnp.zeros_like(wf_pad)
    wf_pad[:VARS] = wf_ref[...]

    scale_row = gain_ref[...] * (1.0 + pert_ref[...].astype(F32))

    def norm_own(step, carry):
        rows = aligned(step, 64)
        normed_ref[rows] = normalise(x_ref[rows], scale_row)
        return carry

    for part in range(4):
        x_copy(part).wait()
        if part < 3:
            w_copy(part).start()
        else:
            wproj_copy.start()
        lax.fori_loop(4 * part, 4 * part + 4, norm_own, 0, unroll=4)

    lane = lax.broadcasted_iota(jnp.int32, (HALF, HALF), 1)
    even_lane = lane < HEAD_DIM

    def put_q(q, pair):
        for b in range(ROWS // BLOCK):
            for g in range(2):
                part = q[b * BLOCK + g * HALF : b * BLOCK + (g + 1) * HALF]
                q_ref[b, pair, g, :HALF] = jnp.where(even_lane, part, 0.0).astype(BF16)
                q_ref[b, pair, g, HALF:] = jnp.where(even_lane, 0.0, part).astype(BF16)

    def put_v(v, pair, at):
        vt = jnp.transpose(v).astype(BF16)
        vt_ref[2 * pair, :HEAD_DIM, at] = vt[:HEAD_DIM]
        vt_ref[2 * pair + 1, :HEAD_DIM, at] = vt[HEAD_DIM:]

    w_copy(0).wait()

    def project_q(tile, carry):
        cols = aligned(tile, 256)
        acc = jnp.dot(normed_ref[...], wqkv_ref[:, cols], preferred_element_type=F32) * 0.125
        put_q(acc[:, :128], 2 * tile)
        put_q(acc[:, 128:], 2 * tile + 1)
        return carry

    lax.fori_loop(0, 4, project_q, 0, unroll=4)
    w_copy(1).wait()

    def project_k(tile, carry):
        cols = aligned(tile, 256)
        acc = jnp.dot(normed_ref[...], wqkv_ref[:, aligned(4 + tile, 256)], preferred_element_type=F32)
        k_ref[BLOCK : BLOCK + ROWS, cols] = acc.astype(BF16)
        return carry

    lax.fori_loop(0, 4, project_k, 0, unroll=4)
    w_copy(2).wait()

    def project_v(tile, carry):
        acc = jnp.dot(normed_ref[...], wqkv_ref[:, aligned(8 + tile, 256)], preferred_element_type=F32)
        at = pl.ds(BLOCK, ROWS)
        put_v(acc[:, :128], 2 * tile, at)
        put_v(acc[:, 128:], 2 * tile + 1, at)
        return carry

    lax.fori_loop(0, 4, project_v, 0, unroll=4)

    def halo_rows():
        to_left.wait_recv()
        to_right.wait_recv()

        def norm_halo(step, carry):
            rows = aligned(step, 64)
            normed_ref[rows] = normalise(halo_ref[step // 4, aligned(step % 4, 64)], scale_row)
            return carry

        lax.fori_loop(0, 8, norm_halo, 0, unroll=4)

        def project_halo(tile, carry):
            normed = normed_ref[: 2 * BLOCK]
            cols = aligned(tile, 256)
            acc = jnp.dot(normed, wqkv_ref[:, aligned(4 + tile, 256)], preferred_element_type=F32)
            k_ref[:BLOCK, cols] = acc[:BLOCK].astype(BF16)
            k_ref[BLOCK + ROWS :, cols] = acc[BLOCK:].astype(BF16)
            acc = jnp.dot(normed, wqkv_ref[:, aligned(8 + tile, 256)], preferred_element_type=F32)
            for half in range(2):
                part = acc[:, half * 128 : (half + 1) * 128]
                put_v(part[:BLOCK], 2 * tile + half, pl.ds(0, BLOCK))
                put_v(part[BLOCK:], 2 * tile + half, pl.ds(BLOCK + ROWS, BLOCK))
            return carry

        lax.fori_loop(0, 4, project_halo, 0, unroll=4)

    S = (s0, s1)
    PB = (p0, p1)
    M = (m0, m1)

    def scores(b, pair, slot, g):
        keys = k_ref[pl.ds(pl.multiple_of(b * BLOCK + g * HALF, HALF), SPAN), pair * 128 : (pair + 1) * 128]
        s = lax.dot_general(keys, q_ref[b, pair, g], NT, preferred_element_type=F32)
        bias = bias_ref[2 * b + g]
        s = s + jnp.concatenate([bias, bias], axis=1)
        S[slot][g] = s
        M[slot][g] = jnp.max(s.reshape(SPAN // 8, 8, 2 * HALF), axis=0)

    def weights(slot, g, h):
        lanes = slice(h * HALF, (h + 1) * HALF)
        top = jnp.max(M[slot][g, :, lanes], axis=0, keepdims=True)
        e = jnp.exp2((S[slot][g, :, lanes] - top) * LOG2E).astype(BF16)
        PB[slot][h, g * HALF : g * HALF + SPAN, g * HALF : (g + 1) * HALF] = e

    def mix(b, pair, slot):
        out = []
        for h in range(2):
            values = vt_ref[2 * pair + h, :, pl.ds(pl.multiple_of(b * BLOCK, BLOCK), 3 * BLOCK)]
            o = jnp.dot(values, PB[slot][h], preferred_element_type=F32)
            out.append(o[:HEAD_DIM] / o[HEAD_DIM : HEAD_DIM + 1])
        both = jnp.concatenate(out, axis=0)
        att_ref[:, pair * 128 : (pair + 1) * 128] = jnp.transpose(both).astype(BF16)

    def attend(b):
        for step in range(PAIRS + 2):
            if step >= 2:
                mix(b, step - 2, step % 2)
            if 1 <= step <= PAIRS:
                for g in range(2):
                    for h in range(2):
                        weights((step - 1) % 2, g, h)
            if step < PAIRS:
                for g in range(2):
                    scores(b, step, step % 2, g)

    def out_copy(order, b, step):
        return pltpu.make_async_remote_copy(
            src_ref=gat_ref.at[ens, b],
            dst_ref=gat_ref.at[ens, b],
            send_sem=out_send.at[order, step - 1],
            recv_sem=out_recv.at[order, step - 1],
            device_id={"ens": (ens + step) % ens_size},
            device_id_type=MESH,
        )

    def in_copy(order, b, step):
        source = (ens + ens_size - step) % ens_size
        return pltpu.make_async_remote_copy(
            src_ref=gat_ref.at[source, b],
            dst_ref=gat_ref.at[source, b],
            send_sem=out_send.at[order, step - 1],
            recv_sem=out_recv.at[order, step - 1],
            device_id={"ens": (ens + step) % ens_size},
            device_id_type=MESH,
        )

    def live_row(b):
        slot = lax.broadcasted_iota(jnp.int32, (1, BLOCK), 1) + b * BLOCK
        return jnp.where(slot < own_count, 1.0, 0.0)

    def decode(order, b):
        rows = aligned(b, BLOCK)
        mixed = jnp.dot(att_ref[...], wproj_ref[...], preferred_element_type=F32)
        updated = (x_ref[rows].astype(F32) + mixed).astype(BF16)
        fields = lax.dot_general(wf_pad[...], updated, NT, preferred_element_type=F32)
        fields = (fields * live_row(b)).astype(BF16)
        gat_ref[ens, b] = fields
        pred_ref[0, :, rows] = fields[:VARS]
        for step in range(1, ens_size):
            out_copy(order, b, step).start()

    def score_rows(b, start, count, live):
        cols = aligned(b, BLOCK)
        rows = pl.ds(start, count)
        tile = pl.ds(start, 16)
        f = [gat_ref[m, b, tile, :].astype(F32)[:count] for m in range(ens_size)]
        mine = gat_ref[ens, b, tile, :].astype(F32)[:count]
        truth = obs_ref[rows, cols]

        def size(d):
            square = d * d + SMOOTH_SQ
            inverse = lax.rsqrt(square)
            return square * inverse, inverse

        to_truth = size(f[0] - truth)[0]
        for m in range(1, ens_size):
            to_truth = to_truth + size(f[m] - truth)[0]
        spread = None
        for m in range(ens_size):
            for other in range(m):
                term = size(f[m] - f[other])[0]
                spread = term if spread is None else spread + term
        grad = None
        for other in range(ens_size):
            d = mine - f[other]
            term = d * size(d)[1]
            grad = term if grad is None else grad + term
        d = mine - truth
        pull = d * size(d)[1]
        score_ref[rows, cols] = live * (
            to_truth * (1.0 / ens_size)
            - ((1.0 - EPS_FAIR) / (ens_size * (ens_size - 1))) * spread
        )
        deriv_ref[rows, 0, cols] = live * (pull - ((1.0 - EPS_FAIR) / (ens_size - 1)) * grad)

    def score(order, b):
        for step in range(1, ens_size):
            in_copy(order, b, step).wait_recv()
        live = live_row(b)

        def some(r, carry):
            score_rows(b, pl.multiple_of(r * 16, 16), 16, live)
            return carry

        lax.fori_loop(0, VARS // 16, some, 0, unroll=2)
        score_rows(b, (VARS // 16) * 16, VARS % 16, live)

    wproj_copy.wait()

    def block_at(order):
        return (order + 1) % 3 + 2 * (order // 3)

    def one_block(order, carry):
        b = block_at(order)

        @pl.when(order == 2)
        def _():
            halo_rows()

        attend(b)
        decode(order, b)

        @pl.when(order >= 2)
        def _():
            score(order - 2, block_at(order - 2))

        return carry

    lax.fori_loop(0, 4, one_block, 0)
    score(2, 0)
    score(3, 3)

    to_left.wait_send()
    to_right.wait_send()

    def sent(order, carry):
        for step in range(1, ens_size):
            out_copy(order, block_at(order), step).wait_send()
        return carry

    lax.fori_loop(0, 4, sent, 0)


def hand_over(pred_in, score_in, deriv_in, pred_out, score_out, deriv_out, pred, score, deriv, in_sem, out_sem):
    paths = ((pred_in, pred, pred_out), (score_in, score, score_out), (deriv_in, deriv, deriv_out))
    reads = [pltpu.make_async_copy(p[0], p[1], in_sem.at[i]) for i, p in enumerate(paths)]
    writes = [pltpu.make_async_copy(p[1], p[2], out_sem.at[i]) for i, p in enumerate(paths)]
    for read in reads:
        read.start()
    for read, write in zip(reads, writes):
        read.wait()
        write.start()
    for write in writes:
        write.wait()


def on_device(x, pert, gain, wqkv, wproj, wf, obs, counts):
    vmem = pl.BlockSpec(memory_space=pltpu.VMEM)
    smem = pl.BlockSpec(memory_space=pltpu.SMEM)
    hbm = pl.BlockSpec(memory_space=pl.ANY)
    dma = pltpu.SemaphoreType.DMA
    pred, score, deriv = pl.pallas_call(
        kernel,
        out_shape=(
            jax.ShapeDtypeStruct((1, VARS, ROWS), BF16),
            jax.ShapeDtypeStruct((VARS, ROWS), F32),
            jax.ShapeDtypeStruct((VARS, 1, ROWS), F32),
        ),
        in_specs=[smem, hbm, vmem, vmem, hbm, hbm, vmem, vmem],
        out_specs=(vmem, vmem, vmem),
        scratch_shapes=[
            pltpu.VMEM((ROWS, C), BF16),
            pltpu.VMEM((2, BLOCK, C), BF16),
            pltpu.VMEM((C, 3 * C), BF16),
            pltpu.VMEM((C, C), BF16),
            pltpu.VMEM((VPAD, C), BF16),
            pltpu.VMEM((ROWS, C), BF16),
            pltpu.VMEM((4, PAIRS, 2, 2 * HALF, 128), BF16),
            pltpu.VMEM((EXT, C), BF16),
            pltpu.VMEM((HEADS, V_ROWS, EXT), BF16),
            pltpu.VMEM((ROWS // HALF, SPAN, HALF), F32),
            pltpu.VMEM((2, SPAN, 2 * HALF), F32),
            pltpu.VMEM((2, SPAN, 2 * HALF), F32),
            pltpu.VMEM((2, 3 * BLOCK, BLOCK), BF16),
            pltpu.VMEM((2, 3 * BLOCK, BLOCK), BF16),
            pltpu.VMEM((2, 8, 2 * HALF), F32),
            pltpu.VMEM((2, 8, 2 * HALF), F32),
            pltpu.VMEM((BLOCK, C), BF16),
            pltpu.VMEM((MEMBERS, 4, VPAD, BLOCK), BF16),
            dma((4,)),
            dma((4,)),
            dma((2,)),
            dma((2,)),
            dma((4, MEMBERS - 1)),
            dma((4, MEMBERS - 1)),
        ],
        compiler_params=pltpu.CompilerParams(
            collective_id=0, has_side_effects=True, vmem_limit_bytes=56 * 2**20
        ),
        cost_estimate=pl.CostEstimate(flops=20_000_000_000, bytes_accessed=14_000_000, transcendentals=13_000_000),
    )(counts, x, pert, gain.reshape(1, C), wqkv, wproj, wf.T, obs)
    pred, score, deriv = pl.pallas_call(
        hand_over,
        out_shape=(
            jax.ShapeDtypeStruct((1, VARS, ROWS), BF16),
            jax.ShapeDtypeStruct((VARS, ROWS), F32),
            jax.ShapeDtypeStruct((VARS, 1, ROWS), F32),
        ),
        in_specs=[hbm] * 3,
        out_specs=(hbm,) * 3,
        scratch_shapes=[
            pltpu.VMEM((1, VARS, ROWS), BF16),
            pltpu.VMEM((VARS, ROWS), F32),
            pltpu.VMEM((VARS, 1, ROWS), F32),
            dma((3,)),
            dma((3,)),
        ],
        compiler_params=pltpu.CompilerParams(vmem_limit_bytes=60 * 2**20),
    )(pred, score, deriv)
    return pred, score, jnp.transpose(deriv, (1, 0, 2))


def solution(mesh):
    return jax.shard_map(
        on_device,
        mesh=mesh,
        in_specs=(P("ens", "node", None), P("ens", None), P(), P(), P(), P(), P(None, "node"), P()),
        out_specs=(P("ens", None, "node"), P(None, "node"), P("ens", None, "node")),
        check_vma=False,
    )
```

```python
import jax
import jax.numpy as jnp
from jax import lax
from jax.experimental import pallas as pl
from jax.experimental.pallas import tpu as pltpu
from jax.sharding import PartitionSpec as P

C = 1024
HEADS = 16
HEAD_DIM = 64
PAIRS = HEADS // 2
ROWS = 1024
BLOCK = 256
HALF = 128
EXT = ROWS + 2 * BLOCK
SPAN = 640
VARS = 100
VPAD = 112
MEMBERS = 8
V_ROWS = 80

SMOOTH_SQ = 0.01
ALPHA_FAIR = 0.95
EPS_FAIR = (1.0 - ALPHA_FAIR) / MEMBERS
LOG2E = 1.4426950408889634
DECODE_AT = 5
MASKED = -1e30

F32 = jnp.float32
BF16 = jnp.bfloat16
NT = (((1,), (1,)), ((), ()))
MESH = pl.DeviceIdType.MESH


def aligned(index, width):
    return pl.ds(pl.multiple_of(index * width, width), width)


def normalise(x, scale_row):
    x32 = x.astype(F32)
    mean = jnp.mean(x32, axis=-1, keepdims=True)
    centred = x32 - mean
    var = jnp.mean(centred * centred, axis=-1, keepdims=True)
    return (centred * lax.rsqrt(var + 1e-5) * scale_row).astype(BF16)


def kernel(
    counts_ref,
    x_hbm,
    pert_ref,
    gain_ref,
    wqkv_hbm,
    wproj_hbm,
    wf_hbm,
    obs_hbm,
    pred_ref,
    score_ref,
    deriv_ref,
    x_ref,
    halo_ref,
    wqkv_ref,
    wproj_ref,
    wf_pad,
    wf_ref,
    obs_ref,
    normed_ref,
    q_ref,
    k_ref,
    vt_ref,
    bias_ref,
    s0,
    s1,
    s2,
    p0,
    p1,
    p2,
    m0,
    m1,
    m2,
    att_ref,
    gat_ref,
    x_sem,
    w_sem,
    halo_send,
    halo_recv,
    out_send,
    out_recv,
):
    ens = lax.axis_index("ens")
    node = lax.axis_index("node")
    ens_size = MEMBERS
    nodes = lax.axis_size("node")
    left = (node + nodes - 1) % nodes
    right = (node + 1) % nodes

    barrier = pltpu.get_barrier_semaphore()
    for near in (left, right):
        pl.semaphore_signal(barrier, inc=1, device_id={"node": near}, device_id_type=MESH)
    for step in range(1, ens_size):
        pl.semaphore_signal(
            barrier, inc=1, device_id={"ens": (ens + step) % ens_size}, device_id_type=MESH
        )

    def x_copy(part):
        rows = pl.ds(part * BLOCK, BLOCK)
        return pltpu.make_async_copy(x_hbm.at[0, rows], x_ref.at[rows], x_sem.at[part])

    def w_copy(part):
        cols = pl.ds(part * C, C)
        return pltpu.make_async_copy(wqkv_hbm.at[:, cols], wqkv_ref.at[:, cols], w_sem.at[part])

    wf_copy = pltpu.make_async_copy(wf_hbm, wf_ref, w_sem.at[4])
    obs_copy = pltpu.make_async_copy(obs_hbm, obs_ref, w_sem.at[5])
    wproj_copy = pltpu.make_async_copy(wproj_hbm, wproj_ref, w_sem.at[3])
    for part in range(4):
        x_copy(part).start()

    pl.semaphore_wait(barrier, ens_size + 1)

    odd = node % 2
    near = (node + nodes + 1 - 2 * odd) % nodes
    far = (node + nodes - 1 + 2 * odd) % nodes
    near_end = (BLOCK + ROWS) * (1 - odd)
    far_end = (BLOCK + ROWS) * odd
    x_halo = pltpu.make_async_remote_copy(
        src_ref=x_hbm.at[0, pl.ds(pl.multiple_of((ROWS - BLOCK) * odd, BLOCK), BLOCK)],
        dst_ref=halo_ref,
        send_sem=halo_send.at[0],
        recv_sem=halo_recv.at[0],
        device_id={"node": far},
        device_id_type=MESH,
    )
    x_halo.start()

    own_edge = ROWS - (ROWS - BLOCK) * odd

    def k_copy(start, end):
        return pltpu.make_async_remote_copy(
            src_ref=k_ref.at[pl.ds(pl.multiple_of(start, BLOCK), BLOCK)],
            dst_ref=k_ref.at[pl.ds(pl.multiple_of(end, BLOCK), BLOCK)],
            send_sem=halo_send.at[1],
            recv_sem=halo_recv.at[1],
            device_id={"node": near},
            device_id_type=MESH,
        )

    def v_copy(start, end):
        return pltpu.make_async_remote_copy(
            src_ref=vt_ref.at[:, pl.ds(0, HEAD_DIM), pl.ds(pl.multiple_of(start, BLOCK), BLOCK)],
            dst_ref=vt_ref.at[:, pl.ds(0, HEAD_DIM), pl.ds(pl.multiple_of(end, BLOCK), BLOCK)],
            send_sem=halo_send.at[2],
            recv_sem=halo_recv.at[2],
            device_id={"node": near},
            device_id_type=MESH,
        )

    k_send, v_send = k_copy(own_edge, far_end), v_copy(own_edge, far_end)
    k_take, v_take = k_copy(near_end, near_end), v_copy(near_end, near_end)

    own_count = counts_ref[node]
    low_count = jnp.where(node > 0, counts_ref[(node + nodes - 1) % nodes], 0)
    high_count = jnp.where(node < nodes - 1, counts_ref[(node + 1) % nodes], 0)
    key = lax.broadcasted_iota(jnp.int32, (SPAN, HALF), 0)
    query = lax.broadcasted_iota(jnp.int32, (SPAN, HALF), 1)
    ahead = key - query
    in_window = (ahead >= 0) & (ahead < 2 * BLOCK)
    itself = ahead == BLOCK

    def make_bias(t, carry):
        place = key + t * HALF
        end = jnp.where(
            place < BLOCK,
            low_count - (ROWS - BLOCK),
            jnp.where(place < BLOCK + ROWS, own_count + BLOCK, high_count + (BLOCK + ROWS)),
        )
        allowed = in_window & ((place < end) | itself)
        bias_ref[t] = jnp.where(allowed, 0.0, MASKED)
        return carry

    lax.fori_loop(0, ROWS // HALF, make_bias, 0)
    for p in (p0, p1, p2):
        p[...] = jnp.zeros_like(p)
    row = lax.broadcasted_iota(jnp.int32, (V_ROWS - HEAD_DIM, EXT), 0)
    tail = jnp.where(row == 0, 1.0, 0.0).astype(BF16)
    for head in range(HEADS):
        vt_ref[head, HEAD_DIM:V_ROWS, :] = tail

    scale_row = gain_ref[...] * (1.0 + pert_ref[...].astype(F32))

    def norm_own(step, carry):
        rows = aligned(step, 64)
        normed_ref[rows] = normalise(x_ref[rows], scale_row)
        return carry

    for part in range(4):
        x_copy(part).wait()
        if part < 3:
            w_copy(part).start()
        else:
            wproj_copy.start()
            wf_copy.start()
            obs_copy.start()
        lax.fori_loop(4 * part, 4 * part + 4, norm_own, 0, unroll=4)

    lane = lax.broadcasted_iota(jnp.int32, (HALF, HALF), 1)
    even_lane = lane < HEAD_DIM

    def put_q(q, pair):
        for b in range(ROWS // BLOCK):
            for g in range(2):
                part = q[b * BLOCK + g * HALF : b * BLOCK + (g + 1) * HALF]
                q_ref[b, pair, g, :HALF] = jnp.where(even_lane, part, 0.0).astype(BF16)
                q_ref[b, pair, g, HALF:] = jnp.where(even_lane, 0.0, part).astype(BF16)

    def put_v(v, pair, at):
        vt = jnp.transpose(v.astype(BF16))
        vt_ref[2 * pair, :HEAD_DIM, at] = vt[:HEAD_DIM]
        vt_ref[2 * pair + 1, :HEAD_DIM, at] = vt[HEAD_DIM:]

    w_copy(0).wait()

    def project_q(tile, carry):
        cols = aligned(tile, 256)
        acc = jnp.dot(normed_ref[...], wqkv_ref[:, cols], preferred_element_type=F32) * 0.125
        put_q(acc[:, :128], 2 * tile)
        put_q(acc[:, 128:], 2 * tile + 1)
        return carry

    lax.fori_loop(0, 4, project_q, 0, unroll=4)
    w_copy(1).wait()

    def project_k(tile, carry):
        cols = aligned(tile, 256)
        acc = jnp.dot(normed_ref[...], wqkv_ref[:, aligned(4 + tile, 256)], preferred_element_type=F32)
        k_ref[BLOCK : BLOCK + ROWS, cols] = acc.astype(BF16)
        return carry

    lax.fori_loop(0, 4, project_k, 0, unroll=4)
    k_send.start()
    w_copy(2).wait()

    def project_v(tile, carry):
        acc = jnp.dot(normed_ref[...], wqkv_ref[:, aligned(8 + tile, 256)], preferred_element_type=F32)
        at = pl.ds(BLOCK, ROWS)
        put_v(acc[:, :128], 2 * tile, at)
        put_v(acc[:, 128:], 2 * tile + 1, at)
        return carry

    lax.fori_loop(0, 4, project_v, 0, unroll=4)
    v_send.start()

    def halo_rows():
        x_halo.wait_recv()

        def norm_halo(step, carry):
            rows = aligned(step, 64)
            normed_ref[rows] = normalise(halo_ref[rows], scale_row)
            return carry

        lax.fori_loop(0, 4, norm_halo, 0, unroll=4)
        end = pl.ds(pl.multiple_of(far_end, BLOCK), BLOCK)

        def project_halo(tile, carry):
            normed = normed_ref[:BLOCK]
            acc = jnp.dot(normed, wqkv_ref[:, aligned(4 + tile, 256)], preferred_element_type=F32)
            k_ref[end, aligned(tile, 256)] = acc.astype(BF16)
            acc = jnp.dot(normed, wqkv_ref[:, aligned(8 + tile, 256)], preferred_element_type=F32)
            put_v(acc[:, :128], 2 * tile, end)
            put_v(acc[:, 128:], 2 * tile + 1, end)
            return carry

        lax.fori_loop(0, 4, project_halo, 0, unroll=4)
        k_take.wait_recv()
        v_take.wait_recv()

    S = (s0, s1, s2)
    PB = (p0, p1, p2)
    M = (m0, m1, m2)

    def scores(b, pair, slot, g):
        keys = k_ref[pl.ds(pl.multiple_of(b * BLOCK + g * HALF, HALF), SPAN), pair * 128 : (pair + 1) * 128]
        s = lax.dot_general(keys, q_ref[b, pair, g], NT, preferred_element_type=F32)
        bias = bias_ref[2 * b + g]
        s = s + jnp.concatenate([bias, bias], axis=1)
        S[slot][g] = s
        M[slot][g] = jnp.max(s.reshape(SPAN // 8, 8, 2 * HALF), axis=0)

    def weights(slot, g, h):
        lanes = slice(h * HALF, (h + 1) * HALF)
        top = jnp.max(M[slot][g, :, lanes], axis=0, keepdims=True)
        e = jnp.exp2((S[slot][g, :, lanes] - top) * LOG2E).astype(BF16)
        PB[slot][h, g * HALF : g * HALF + SPAN, g * HALF : (g + 1) * HALF] = e

    def mix(b, pair, slot, h):
        values = vt_ref[2 * pair + h, :, pl.ds(pl.multiple_of(b * BLOCK, BLOCK), 3 * BLOCK)]
        o = jnp.dot(values, PB[slot][h], preferred_element_type=F32)
        return o[:HEAD_DIM] * (1.0 / o[HEAD_DIM : HEAD_DIM + 1])

    def attend_two(order, blocks):
        units = 2 * PAIRS
        for step in range(units + 4):
            scoring, weighing, mixing = step < units, 0 <= step - 2 < units, 0 <= step - 4
            which, pair = divmod(step, PAIRS)
            which_mix, pair_mix = divmod(step - 4, PAIRS)
            mixed = []
            for g in range(2):
                if scoring:
                    scores(blocks[which], pair, step % 3, g)
                if weighing:
                    for h in range(2):
                        weights((step - 2) % 3, g, h)
                if mixing:
                    mixed.append(mix(blocks[which_mix], pair_mix, (step - 4) % 3, g))
            if mixing:
                both = jnp.concatenate(mixed, axis=0).astype(BF16)
                att_ref[which_mix, :, pair_mix * 128 : (pair_mix + 1) * 128] = jnp.transpose(both)
            if step == PAIRS + DECODE_AT:
                decode(order, blocks[0], 0)
        decode(order + 1, blocks[1], 1)

    def out_copy(order, b, step):
        return pltpu.make_async_remote_copy(
            src_ref=gat_ref.at[ens, b],
            dst_ref=gat_ref.at[ens, b],
            send_sem=out_send.at[order, step - 1],
            recv_sem=out_recv.at[order, step - 1],
            device_id={"ens": (ens + step) % ens_size},
            device_id_type=MESH,
        )

    def in_copy(order, b, step):
        source = (ens + ens_size - step) % ens_size
        return pltpu.make_async_remote_copy(
            src_ref=gat_ref.at[source, b],
            dst_ref=gat_ref.at[source, b],
            send_sem=out_send.at[order, step - 1],
            recv_sem=out_recv.at[order, step - 1],
            device_id={"ens": (ens + step) % ens_size},
            device_id_type=MESH,
        )

    def live_row(b):
        slot = lax.broadcasted_iota(jnp.int32, (1, BLOCK), 1) + b * BLOCK
        return jnp.where(slot < own_count, 1.0, 0.0)

    def decode(order, b, which):
        rows = aligned(b, BLOCK)
        mixed = jnp.dot(att_ref[which], wproj_ref[...], preferred_element_type=F32)
        updated = (x_ref[rows].astype(F32) + mixed).astype(BF16)
        fields = lax.dot_general(wf_pad[...], updated, NT, preferred_element_type=F32)
        fields = (fields * live_row(b)).astype(BF16)
        gat_ref[ens, b] = fields
        pred_ref[0, :, rows] = fields[:VARS]
        for step in range(1, ens_size):
            out_copy(order, b, step).start()

    def score_rows(b, start, count, live):
        cols = aligned(b, BLOCK)
        rows = pl.ds(start, count)
        tile = pl.ds(start, 16)
        f = [gat_ref[m, b, tile, :].astype(F32)[:count] for m in range(ens_size)]
        mine = gat_ref[ens, b, tile, :].astype(F32)[:count]
        truth = obs_ref[rows, cols]

        def size(d):
            square = d * d + SMOOTH_SQ
            inverse = lax.rsqrt(square)
            return square * inverse, inverse

        to_truth = size(f[0] - truth)[0]
        for m in range(1, ens_size):
            to_truth = to_truth + size(f[m] - truth)[0]
        spread = None
        for m in range(ens_size):
            for other in range(m):
                term = size(f[m] - f[other])[0]
                spread = term if spread is None else spread + term
        grad = None
        for other in range(ens_size):
            d = mine - f[other]
            term = d * size(d)[1]
            grad = term if grad is None else grad + term
        d = mine - truth
        pull = d * size(d)[1]
        score_ref[rows, cols] = live * (
            to_truth * (1.0 / ens_size)
            - ((1.0 - EPS_FAIR) / (ens_size * (ens_size - 1))) * spread
        )
        deriv_ref[rows, 0, cols] = live * (pull - ((1.0 - EPS_FAIR) / (ens_size - 1)) * grad)

    def score(order, b):
        for step in range(1, ens_size):
            in_copy(order, b, step).wait_recv()
        live = live_row(b)

        def some(r, carry):
            score_rows(b, pl.multiple_of(r * 16, 16), 16, live)
            return carry

        lax.fori_loop(0, VARS // 16, some, 0, unroll=2)
        score_rows(b, (VARS // 16) * 16, VARS % 16, live)

    wproj_copy.wait()
    wf_copy.wait()
    wf_pad[...] = jnp.zeros_like(wf_pad)
    wf_pad[:VARS] = wf_ref[...]

    def two_blocks(phase, carry):
        @pl.when(phase == 1)
        def _():
            halo_rows()

        attend_two(2 * phase, (1 - phase, 2 + phase))
        return carry

    lax.fori_loop(0, 2, two_blocks, 0)
    obs_copy.wait()
    for order, b in enumerate((1, 2, 0, 3)):
        score(order, b)

    x_halo.wait_send()
    k_send.wait_send()
    v_send.wait_send()

    for order, b in enumerate((1, 2, 0, 3)):
        for step in range(1, ens_size):
            out_copy(order, b, step).wait_send()


def hand_over(pred_in, score_in, deriv_in, pred_out, score_out, deriv_out, pred, score, deriv, in_sem, out_sem):
    paths = ((pred_in, pred, pred_out), (score_in, score, score_out), (deriv_in, deriv, deriv_out))
    reads = [pltpu.make_async_copy(p[0], p[1], in_sem.at[i]) for i, p in enumerate(paths)]
    writes = [pltpu.make_async_copy(p[1], p[2], out_sem.at[i]) for i, p in enumerate(paths)]
    for read in reads:
        read.start()
    for read, write in zip(reads, writes):
        read.wait()
        write.start()
    for write in writes:
        write.wait()


def on_device(x, pert, gain, wqkv, wproj, wf, obs, counts):
    vmem = pl.BlockSpec(memory_space=pltpu.VMEM)
    smem = pl.BlockSpec(memory_space=pltpu.SMEM)
    hbm = pl.BlockSpec(memory_space=pl.ANY)
    dma = pltpu.SemaphoreType.DMA
    pred, score, deriv = pl.pallas_call(
        kernel,
        out_shape=(
            jax.ShapeDtypeStruct((1, VARS, ROWS), BF16),
            jax.ShapeDtypeStruct((VARS, ROWS), F32),
            jax.ShapeDtypeStruct((VARS, 1, ROWS), F32),
        ),
        in_specs=[smem, hbm, vmem, vmem, hbm, hbm, hbm, hbm],
        out_specs=(vmem, vmem, vmem),
        scratch_shapes=[
            pltpu.VMEM((ROWS, C), BF16),
            pltpu.VMEM((BLOCK, C), BF16),
            pltpu.VMEM((C, 3 * C), BF16),
            pltpu.VMEM((C, C), BF16),
            pltpu.VMEM((VPAD, C), BF16),
            pltpu.VMEM((VARS, C), BF16),
            pltpu.VMEM((VARS, ROWS), F32),
            pltpu.VMEM((ROWS, C), BF16),
            pltpu.VMEM((4, PAIRS, 2, 2 * HALF, 128), BF16),
            pltpu.VMEM((EXT, C), BF16),
            pltpu.VMEM((HEADS, V_ROWS, EXT), BF16),
            pltpu.VMEM((ROWS // HALF, SPAN, HALF), F32),
            pltpu.VMEM((2, SPAN, 2 * HALF), F32),
            pltpu.VMEM((2, SPAN, 2 * HALF), F32),
            pltpu.VMEM((2, SPAN, 2 * HALF), F32),
            pltpu.VMEM((2, 3 * BLOCK, BLOCK), BF16),
            pltpu.VMEM((2, 3 * BLOCK, BLOCK), BF16),
            pltpu.VMEM((2, 3 * BLOCK, BLOCK), BF16),
            pltpu.VMEM((2, 8, 2 * HALF), F32),
            pltpu.VMEM((2, 8, 2 * HALF), F32),
            pltpu.VMEM((2, 8, 2 * HALF), F32),
            pltpu.VMEM((2, BLOCK, C), BF16),
            pltpu.VMEM((MEMBERS, 4, VPAD, BLOCK), BF16),
            dma((4,)),
            dma((6,)),
            dma((3,)),
            dma((3,)),
            dma((4, MEMBERS - 1)),
            dma((4, MEMBERS - 1)),
        ],
        compiler_params=pltpu.CompilerParams(
            collective_id=0, has_side_effects=True, vmem_limit_bytes=56 * 2**20
        ),
        cost_estimate=pl.CostEstimate(flops=20_000_000_000, bytes_accessed=14_000_000, transcendentals=13_000_000),
    )(counts, x, pert, gain.reshape(1, C), wqkv, wproj, wf.T, obs)
    pred, score, deriv = pl.pallas_call(
        hand_over,
        out_shape=(
            jax.ShapeDtypeStruct((1, VARS, ROWS), BF16),
            jax.ShapeDtypeStruct((VARS, ROWS), F32),
            jax.ShapeDtypeStruct((VARS, 1, ROWS), F32),
        ),
        in_specs=[hbm] * 3,
        out_specs=(hbm,) * 3,
        scratch_shapes=[
            pltpu.VMEM((1, VARS, ROWS), BF16),
            pltpu.VMEM((VARS, ROWS), F32),
            pltpu.VMEM((VARS, 1, ROWS), F32),
            dma((3,)),
            dma((3,)),
        ],
        compiler_params=pltpu.CompilerParams(vmem_limit_bytes=60 * 2**20),
    )(pred, score, deriv)
    return pred, score, jnp.transpose(deriv, (1, 0, 2))


def solution(mesh):
    return jax.shard_map(
        on_device,
        mesh=mesh,
        in_specs=(P("ens", "node", None), P("ens", None), P(), P(), P(), P(), P(None, "node"), P()),
        out_specs=(P("ens", None, "node"), P(None, "node"), P("ens", None, "node")),
        check_vma=False,
    )
```

```python
import jax
import jax.numpy as jnp
from jax import lax
from jax.experimental import pallas as pl
from jax.experimental.pallas import tpu as pltpu
from jax.sharding import PartitionSpec as P

C = 1024
HEADS = 16
HEAD_DIM = 64
PAIRS = HEADS // 2
ROWS = 1024
BLOCK = 256
HALF = 128
EXT = ROWS + 2 * BLOCK
SPAN = 640
VARS = 100
VPAD = 112
MEMBERS = 8
V_ROWS = 80

SMOOTH_SQ = 0.01
ALPHA_FAIR = 0.95
EPS_FAIR = (1.0 - ALPHA_FAIR) / MEMBERS
LOG2E = 1.4426950408889634
DECODE_AT = 3
MASKED = -1e30

F32 = jnp.float32
BF16 = jnp.bfloat16
NT = (((1,), (1,)), ((), ()))
MESH = pl.DeviceIdType.MESH


def aligned(index, width):
    return pl.ds(pl.multiple_of(index * width, width), width)


def normalise(x, scale_row):
    x32 = x.astype(F32)
    mean = jnp.mean(x32, axis=-1, keepdims=True)
    centred = x32 - mean
    var = jnp.mean(centred * centred, axis=-1, keepdims=True)
    return (centred * lax.rsqrt(var + 1e-5) * scale_row).astype(BF16)


def kernel(
    counts_ref,
    x_hbm,
    pert_ref,
    gain_ref,
    wqkv_hbm,
    wproj_hbm,
    wf_hbm,
    obs_hbm,
    pred_ref,
    score_ref,
    deriv_ref,
    x_ref,
    halo_ref,
    wqkv_ref,
    wproj_ref,
    wf_pad,
    wf_ref,
    obs_ref,
    normed_ref,
    q_ref,
    k_ref,
    vt_ref,
    bias_ref,
    s0,
    s1,
    s2,
    p0,
    p1,
    p2,
    m0,
    m1,
    m2,
    att_ref,
    gat_ref,
    x_sem,
    w_sem,
    halo_send,
    halo_recv,
    out_send,
    out_recv,
):
    ens = lax.axis_index("ens")
    node = lax.axis_index("node")
    ens_size = MEMBERS
    nodes = lax.axis_size("node")
    left = (node + nodes - 1) % nodes
    right = (node + 1) % nodes

    barrier = pltpu.get_barrier_semaphore()
    for near in (left, right):
        pl.semaphore_signal(barrier, inc=1, device_id={"node": near}, device_id_type=MESH)
    for step in range(1, ens_size):
        pl.semaphore_signal(
            barrier, inc=1, device_id={"ens": (ens + step) % ens_size}, device_id_type=MESH
        )

    def x_copy(part):
        rows = pl.ds(part * BLOCK, BLOCK)
        return pltpu.make_async_copy(x_hbm.at[0, rows], x_ref.at[rows], x_sem.at[part])

    def w_copy(part):
        cols = pl.ds(part * C, C)
        return pltpu.make_async_copy(wqkv_hbm.at[:, cols], wqkv_ref.at[:, cols], w_sem.at[part])

    wf_copy = pltpu.make_async_copy(wf_hbm, wf_ref, w_sem.at[4])
    obs_copy = pltpu.make_async_copy(obs_hbm, obs_ref, w_sem.at[5])
    wproj_copy = pltpu.make_async_copy(wproj_hbm, wproj_ref, w_sem.at[3])
    for part in range(4):
        x_copy(part).start()

    pl.semaphore_wait(barrier, ens_size + 1)

    odd = node % 2
    near = (node + nodes + 1 - 2 * odd) % nodes
    far = (node + nodes - 1 + 2 * odd) % nodes
    near_end = (BLOCK + ROWS) * (1 - odd)
    far_end = (BLOCK + ROWS) * odd
    x_halo = pltpu.make_async_remote_copy(
        src_ref=x_hbm.at[0, pl.ds(pl.multiple_of((ROWS - BLOCK) * odd, BLOCK), BLOCK)],
        dst_ref=halo_ref,
        send_sem=halo_send.at[0],
        recv_sem=halo_recv.at[0],
        device_id={"node": far},
        device_id_type=MESH,
    )
    x_halo.start()

    own_edge = ROWS - (ROWS - BLOCK) * odd

    def k_copy(start, end):
        return pltpu.make_async_remote_copy(
            src_ref=k_ref.at[pl.ds(pl.multiple_of(start, BLOCK), BLOCK)],
            dst_ref=k_ref.at[pl.ds(pl.multiple_of(end, BLOCK), BLOCK)],
            send_sem=halo_send.at[1],
            recv_sem=halo_recv.at[1],
            device_id={"node": near},
            device_id_type=MESH,
        )

    def v_copy(start, end):
        return pltpu.make_async_remote_copy(
            src_ref=vt_ref.at[:, pl.ds(0, HEAD_DIM), pl.ds(pl.multiple_of(start, BLOCK), BLOCK)],
            dst_ref=vt_ref.at[:, pl.ds(0, HEAD_DIM), pl.ds(pl.multiple_of(end, BLOCK), BLOCK)],
            send_sem=halo_send.at[2],
            recv_sem=halo_recv.at[2],
            device_id={"node": near},
            device_id_type=MESH,
        )

    k_send, v_send = k_copy(own_edge, far_end), v_copy(own_edge, far_end)
    k_take, v_take = k_copy(near_end, near_end), v_copy(near_end, near_end)

    own_count = counts_ref[node]
    low_count = jnp.where(node > 0, counts_ref[(node + nodes - 1) % nodes], 0)
    high_count = jnp.where(node < nodes - 1, counts_ref[(node + 1) % nodes], 0)
    key = lax.broadcasted_iota(jnp.int32, (SPAN, HALF), 0)
    query = lax.broadcasted_iota(jnp.int32, (SPAN, HALF), 1)
    ahead = key - query
    in_window = (ahead >= 0) & (ahead < 2 * BLOCK)
    itself = ahead == BLOCK

    def make_bias(t, carry):
        place = key + t * HALF
        end = jnp.where(
            place < BLOCK,
            low_count - (ROWS - BLOCK),
            jnp.where(place < BLOCK + ROWS, own_count + BLOCK, high_count + (BLOCK + ROWS)),
        )
        allowed = in_window & ((place < end) | itself)
        bias_ref[t] = jnp.where(allowed, 0.0, MASKED)
        return carry

    lax.fori_loop(0, ROWS // HALF, make_bias, 0)
    for p in (p0, p1, p2):
        p[...] = jnp.zeros_like(p)
    row = lax.broadcasted_iota(jnp.int32, (V_ROWS - HEAD_DIM, EXT), 0)
    tail = jnp.where(row == 0, 1.0, 0.0).astype(BF16)
    for head in range(HEADS):
        vt_ref[head, HEAD_DIM:V_ROWS, :] = tail

    scale_row = gain_ref[...] * (1.0 + pert_ref[...].astype(F32))

    def norm_own(step, carry):
        rows = aligned(step, 64)
        normed_ref[rows] = normalise(x_ref[rows], scale_row)
        return carry

    for part in range(4):
        x_copy(part).wait()
        if part < 3:
            w_copy(part).start()
        else:
            wproj_copy.start()
            wf_copy.start()
            obs_copy.start()
        lax.fori_loop(4 * part, 4 * part + 4, norm_own, 0, unroll=4)

    lane = lax.broadcasted_iota(jnp.int32, (HALF, HALF), 1)
    even_lane = lane < HEAD_DIM

    def put_q(q, pair):
        for b in range(ROWS // BLOCK):
            for g in range(2):
                part = q[b * BLOCK + g * HALF : b * BLOCK + (g + 1) * HALF]
                q_ref[b, pair, g, :HALF] = jnp.where(even_lane, part, 0.0).astype(BF16)
                q_ref[b, pair, g, HALF:] = jnp.where(even_lane, 0.0, part).astype(BF16)

    def put_v(v, pair, at):
        vt = jnp.transpose(v.astype(BF16))
        vt_ref[2 * pair, :HEAD_DIM, at] = vt[:HEAD_DIM]
        vt_ref[2 * pair + 1, :HEAD_DIM, at] = vt[HEAD_DIM:]

    w_copy(0).wait()

    def project_q(tile, carry):
        cols = aligned(tile, 256)
        acc = jnp.dot(normed_ref[...], wqkv_ref[:, cols], preferred_element_type=F32) * 0.125
        put_q(acc[:, :128], 2 * tile)
        put_q(acc[:, 128:], 2 * tile + 1)
        return carry

    lax.fori_loop(0, 4, project_q, 0, unroll=4)
    w_copy(1).wait()

    def project_k(tile, carry):
        cols = aligned(tile, 256)
        acc = jnp.dot(normed_ref[...], wqkv_ref[:, aligned(4 + tile, 256)], preferred_element_type=F32)
        k_ref[BLOCK : BLOCK + ROWS, cols] = acc.astype(BF16)
        return carry

    lax.fori_loop(0, 4, project_k, 0, unroll=4)
    k_send.start()
    w_copy(2).wait()

    def project_v(tile, carry):
        acc = jnp.dot(normed_ref[...], wqkv_ref[:, aligned(8 + tile, 256)], preferred_element_type=F32)
        at = pl.ds(BLOCK, ROWS)
        put_v(acc[:, :128], 2 * tile, at)
        put_v(acc[:, 128:], 2 * tile + 1, at)
        return carry

    lax.fori_loop(0, 4, project_v, 0, unroll=4)
    v_send.start()

    def halo_rows():
        x_halo.wait_recv()

        def norm_halo(step, carry):
            rows = aligned(step, 64)
            normed_ref[rows] = normalise(halo_ref[rows], scale_row)
            return carry

        lax.fori_loop(0, 4, norm_halo, 0, unroll=4)
        end = pl.ds(pl.multiple_of(far_end, BLOCK), BLOCK)

        def project_halo(tile, carry):
            normed = normed_ref[:BLOCK]
            acc = jnp.dot(normed, wqkv_ref[:, aligned(4 + tile, 256)], preferred_element_type=F32)
            k_ref[end, aligned(tile, 256)] = acc.astype(BF16)
            acc = jnp.dot(normed, wqkv_ref[:, aligned(8 + tile, 256)], preferred_element_type=F32)
            put_v(acc[:, :128], 2 * tile, end)
            put_v(acc[:, 128:], 2 * tile + 1, end)
            return carry

        lax.fori_loop(0, 4, project_halo, 0, unroll=4)
        k_take.wait_recv()
        v_take.wait_recv()

    S = (s0, s1, s2)
    PB = (p0, p1, p2)
    M = (m0, m1, m2)

    def scores(b, pair, slot, g):
        keys = k_ref[pl.ds(pl.multiple_of(b * BLOCK + g * HALF, HALF), SPAN), pair * 128 : (pair + 1) * 128]
        s = lax.dot_general(keys, q_ref[b, pair, g], NT, preferred_element_type=F32)
        bias = bias_ref[2 * b + g]
        s = s + jnp.concatenate([bias, bias], axis=1)
        S[slot][g] = s
        M[slot][g] = jnp.max(s.reshape(SPAN // 8, 8, 2 * HALF), axis=0)

    def weights(slot, g, h):
        lanes = slice(h * HALF, (h + 1) * HALF)
        top = jnp.max(M[slot][g, :, lanes], axis=0, keepdims=True)
        e = jnp.exp2((S[slot][g, :, lanes] - top) * LOG2E).astype(BF16)
        PB[slot][h, g * HALF : g * HALF + SPAN, g * HALF : (g + 1) * HALF] = e

    def mix(b, pair, slot, h):
        values = vt_ref[2 * pair + h, :, pl.ds(pl.multiple_of(b * BLOCK, BLOCK), 3 * BLOCK)]
        o = jnp.dot(values, PB[slot][h], preferred_element_type=F32)
        return o[:HEAD_DIM] * (1.0 / o[HEAD_DIM : HEAD_DIM + 1])

    def attend_two(order, blocks):
        units = 2 * PAIRS
        for step in range(units + 4):
            scoring, weighing, mixing = step < units, 0 <= step - 2 < units, 0 <= step - 4
            which, pair = divmod(step, PAIRS)
            which_mix, pair_mix = divmod(step - 4, PAIRS)
            mixed = []
            for g in range(2):
                if scoring:
                    scores(blocks[which], pair, step % 3, g)
                if weighing:
                    for h in range(2):
                        weights((step - 2) % 3, g, h)
                if mixing:
                    mixed.append(mix(blocks[which_mix], pair_mix, (step - 4) % 3, g))
            if mixing:
                both = jnp.concatenate(mixed, axis=0).astype(BF16)
                att_ref[which_mix, :, pair_mix * 128 : (pair_mix + 1) * 128] = jnp.transpose(both)
            if step == PAIRS + DECODE_AT:
                decode(order, blocks[0], 0)
                send_first(order, blocks[0])

                @pl.when(order == 2)
                def _():
                    send_onward(1, 2)

        decode(order + 1, blocks[1], 1)

        @pl.when(order == 0)
        def _():
            send_first(1, 2)

        @pl.when(order == 2)
        def _():
            send_onward(2, 0)
            for step in range(1, ens_size):
                out_copy(3, 3, step).start()

    def out_copy(order, b, step):
        return pltpu.make_async_remote_copy(
            src_ref=gat_ref.at[ens, b],
            dst_ref=gat_ref.at[ens, b],
            send_sem=out_send.at[order, step - 1],
            recv_sem=out_recv.at[order, step - 1],
            device_id={"ens": (ens + step) % ens_size},
            device_id_type=MESH,
        )

    def in_copy(order, b, step):
        source = (ens + ens_size - step) % ens_size
        return pltpu.make_async_remote_copy(
            src_ref=gat_ref.at[source, b],
            dst_ref=gat_ref.at[source, b],
            send_sem=out_send.at[order, step - 1],
            recv_sem=out_recv.at[order, step - 1],
            device_id={"ens": (ens + step) % ens_size},
            device_id_type=MESH,
        )

    y, z = ens // 2, ens % 2
    peers = ens_size // 2
    partner = 2 * y + (1 - z)
    up = 2 * ((y + 1) % peers) + z
    down = 2 * ((y + peers - 1) % peers) + z
    across = 2 * ((y + 2) % peers) + z
    up_other, down_other, across_other = (peer + 1 - 2 * z for peer in (up, down, across))
    first = ((ens, partner), (ens, up), (ens, down), (ens, across))
    onward = ((partner, down), (down, partner), (across, partner))
    arriving = (partner, down, up, across, up_other, down_other, across_other)

    def part_copy(order, b, index, member, target):
        return pltpu.make_async_remote_copy(
            src_ref=gat_ref.at[member, b],
            dst_ref=gat_ref.at[member, b],
            send_sem=out_send.at[order, index],
            recv_sem=out_recv.at[order, index],
            device_id={"ens": target},
            device_id_type=MESH,
        )

    def send_first(order, b):
        for index, (member, target) in enumerate(first):
            part_copy(order, b, index, member, target).start()

    def take(order, b, indices):
        for index in indices:
            part_copy(order, b, index, arriving[index], partner).wait_recv()

    def send_onward(order, b):
        take(order, b, (0, 1, 3))
        for index, (member, target) in enumerate(onward):
            part_copy(order, b, 4 + index, member, target).start()

    def live_row(b):
        slot = lax.broadcasted_iota(jnp.int32, (1, BLOCK), 1) + b * BLOCK
        return jnp.where(slot < own_count, 1.0, 0.0)

    def decode(order, b, which):
        rows = aligned(b, BLOCK)
        mixed = jnp.dot(att_ref[which], wproj_ref[...], preferred_element_type=F32)
        updated = (x_ref[rows].astype(F32) + mixed).astype(BF16)
        fields = lax.dot_general(wf_pad[...], updated, NT, preferred_element_type=F32)
        fields = (fields * live_row(b)).astype(BF16)
        gat_ref[ens, b] = fields
        pred_ref[0, :, rows] = fields[:VARS]

    def score_rows(b, start, count, live):
        cols = aligned(b, BLOCK)
        rows = pl.ds(start, count)
        tile = pl.ds(start, 16)
        f = [gat_ref[m, b, tile, :].astype(F32)[:count] for m in range(ens_size)]
        mine = gat_ref[ens, b, tile, :].astype(F32)[:count]
        truth = obs_ref[rows, cols]

        def size(d):
            square = d * d + SMOOTH_SQ
            inverse = lax.rsqrt(square)
            return square * inverse, inverse

        to_truth = size(f[0] - truth)[0]
        for m in range(1, ens_size):
            to_truth = to_truth + size(f[m] - truth)[0]
        spread = None
        for m in range(ens_size):
            for other in range(m):
                term = size(f[m] - f[other])[0]
                spread = term if spread is None else spread + term
        grad = None
        for other in range(ens_size):
            d = mine - f[other]
            term = d * size(d)[1]
            grad = term if grad is None else grad + term
        d = mine - truth
        pull = d * size(d)[1]
        score_ref[rows, cols] = live * (
            to_truth * (1.0 / ens_size)
            - ((1.0 - EPS_FAIR) / (ens_size * (ens_size - 1))) * spread
        )
        deriv_ref[rows, 0, cols] = live * (pull - ((1.0 - EPS_FAIR) / (ens_size - 1)) * grad)

    def score(order, b):
        if order == 3:
            for step in range(1, ens_size):
                in_copy(order, b, step).wait_recv()
        else:
            take(order, b, (2, 4, 5, 6))
        live = live_row(b)

        def some(r, carry):
            score_rows(b, pl.multiple_of(r * 16, 16), 16, live)
            return carry

        lax.fori_loop(0, VARS // 16, some, 0, unroll=2)
        score_rows(b, (VARS // 16) * 16, VARS % 16, live)

    wproj_copy.wait()
    wf_copy.wait()
    wf_pad[...] = jnp.zeros_like(wf_pad)
    wf_pad[:VARS] = wf_ref[...]

    def two_blocks(phase, carry):
        @pl.when(phase == 1)
        def _():
            halo_rows()
            send_onward(0, 1)

        attend_two(2 * phase, (1 - phase, 2 + phase))
        return carry

    lax.fori_loop(0, 2, two_blocks, 0)
    obs_copy.wait()
    for order, b in enumerate((1, 2, 0, 3)):
        score(order, b)

    x_halo.wait_send()
    k_send.wait_send()
    v_send.wait_send()

    for order, b in enumerate((1, 2, 0, 3)):
        for step in range(1, ens_size):
            if order == 3:
                out_copy(order, b, step).wait_send()
            else:
                member, target = (first + onward)[step - 1]
                part_copy(order, b, step - 1, member, target).wait_send()


def hand_over(pred_in, score_in, deriv_in, pred_out, score_out, deriv_out, pred, score, deriv, in_sem, out_sem):
    paths = ((pred_in, pred, pred_out), (score_in, score, score_out), (deriv_in, deriv, deriv_out))
    reads = [pltpu.make_async_copy(p[0], p[1], in_sem.at[i]) for i, p in enumerate(paths)]
    writes = [pltpu.make_async_copy(p[1], p[2], out_sem.at[i]) for i, p in enumerate(paths)]
    for read in reads:
        read.start()
    for read, write in zip(reads, writes):
        read.wait()
        write.start()
    for write in writes:
        write.wait()


def on_device(x, pert, gain, wqkv, wproj, wf, obs, counts):
    vmem = pl.BlockSpec(memory_space=pltpu.VMEM)
    smem = pl.BlockSpec(memory_space=pltpu.SMEM)
    hbm = pl.BlockSpec(memory_space=pl.ANY)
    dma = pltpu.SemaphoreType.DMA
    pred, score, deriv = pl.pallas_call(
        kernel,
        out_shape=(
            jax.ShapeDtypeStruct((1, VARS, ROWS), BF16),
            jax.ShapeDtypeStruct((VARS, ROWS), F32),
            jax.ShapeDtypeStruct((VARS, 1, ROWS), F32),
        ),
        in_specs=[smem, hbm, vmem, vmem, hbm, hbm, hbm, hbm],
        out_specs=(vmem, vmem, vmem),
        scratch_shapes=[
            pltpu.VMEM((ROWS, C), BF16),
            pltpu.VMEM((BLOCK, C), BF16),
            pltpu.VMEM((C, 3 * C), BF16),
            pltpu.VMEM((C, C), BF16),
            pltpu.VMEM((VPAD, C), BF16),
            pltpu.VMEM((VARS, C), BF16),
            pltpu.VMEM((VARS, ROWS), F32),
            pltpu.VMEM((ROWS, C), BF16),
            pltpu.VMEM((4, PAIRS, 2, 2 * HALF, 128), BF16),
            pltpu.VMEM((EXT, C), BF16),
            pltpu.VMEM((HEADS, V_ROWS, EXT), BF16),
            pltpu.VMEM((ROWS // HALF, SPAN, HALF), F32),
            pltpu.VMEM((2, SPAN, 2 * HALF), F32),
            pltpu.VMEM((2, SPAN, 2 * HALF), F32),
            pltpu.VMEM((2, SPAN, 2 * HALF), F32),
            pltpu.VMEM((2, 3 * BLOCK, BLOCK), BF16),
            pltpu.VMEM((2, 3 * BLOCK, BLOCK), BF16),
            pltpu.VMEM((2, 3 * BLOCK, BLOCK), BF16),
            pltpu.VMEM((2, 8, 2 * HALF), F32),
            pltpu.VMEM((2, 8, 2 * HALF), F32),
            pltpu.VMEM((2, 8, 2 * HALF), F32),
            pltpu.VMEM((2, BLOCK, C), BF16),
            pltpu.VMEM((MEMBERS, 4, VPAD, BLOCK), BF16),
            dma((4,)),
            dma((6,)),
            dma((3,)),
            dma((3,)),
            dma((4, MEMBERS - 1)),
            dma((4, MEMBERS - 1)),
        ],
        compiler_params=pltpu.CompilerParams(
            collective_id=0, has_side_effects=True, vmem_limit_bytes=56 * 2**20
        ),
        cost_estimate=pl.CostEstimate(flops=20_000_000_000, bytes_accessed=14_000_000, transcendentals=13_000_000),
    )(counts, x, pert, gain.reshape(1, C), wqkv, wproj, wf.T, obs)
    pred, score, deriv = pl.pallas_call(
        hand_over,
        out_shape=(
            jax.ShapeDtypeStruct((1, VARS, ROWS), BF16),
            jax.ShapeDtypeStruct((VARS, ROWS), F32),
            jax.ShapeDtypeStruct((VARS, 1, ROWS), F32),
        ),
        in_specs=[hbm] * 3,
        out_specs=(hbm,) * 3,
        scratch_shapes=[
            pltpu.VMEM((1, VARS, ROWS), BF16),
            pltpu.VMEM((VARS, ROWS), F32),
            pltpu.VMEM((VARS, 1, ROWS), F32),
            dma((3,)),
            dma((3,)),
        ],
        compiler_params=pltpu.CompilerParams(vmem_limit_bytes=60 * 2**20),
    )(pred, score, deriv)
    return pred, score, jnp.transpose(deriv, (1, 0, 2))


def solution(mesh):
    return jax.shard_map(
        on_device,
        mesh=mesh,
        in_specs=(P("ens", "node", None), P("ens", None), P(), P(), P(), P(), P(None, "node"), P()),
        out_specs=(P("ens", None, "node"), P(None, "node"), P("ens", None, "node")),
        check_vma=False,
    )
```
